256 devices in a mesh: pair: 32 (over y, x, core), win: 8 (over z).
Axes of the slice: x: 4, y: 4, z: 8, core: 2. Of those that a mesh axis runs over, the one named last changes fastest.
Arguments:
- spectra: float32 [2, 8, 6144, 2048], P(None, 'win', 'pair'), may hold values from -400 to 400
- pair_list: int32 [32, 2, 2], replicated, may hold values from 0 to 95, as said below
Outputs:
- stack: float32 [64, 8, 32, 16, 1024], P('pair', 'win')
The draws below stay inside these ranges and needn't reach their ends.
Inputs may be any that keep to these rules, and one draw needn't show every extreme that they name: For each owner q, the 4 blocks listed in pair_list[q] lie on 4 different indices of pair (block k on index k // 3): at most one from any index.
All inputs are finite; a program needn't handle non-finite values.
Results may differ from the reference program's by a relative error of at most 0.0056.
Values may be sent and summed in bfloat16 or wider, within the bound.
A program may use at most 256 MiB of HBM per device.

```python
import jax
import jax.numpy as jnp
from jax import lax

CH = 64
BLK_DEV = 3
PB_DEV = 2
NF = 2048
BAND = 128
NLAG = 1024
WINDOWS = 8
CHANNELS = 6144
SRC_TILE = 32
RCV_TILE = 16
N_PAIR = 32
N_WIN = 8


def draw_spectra(key, part):
    key = jax.random.fold_in(key, 5)
    key_level, key_real = jax.random.split(key)
    shape = (2, WINDOWS, CHANNELS, NF)
    level_shape = (1, WINDOWS, CHANNELS, NF // BAND, 1)
    levels = jnp.exp(jax.random.uniform(key_level, level_shape, jnp.float32, 0.0, jnp.log(30.0)))
    values = jax.random.truncated_normal(key_real, -4.0, 4.0, (2, WINDOWS, CHANNELS, NF // BAND, BAND), jnp.float32)
    return (values * levels).reshape(shape).astype(jnp.float32)


def draw_pair_list(key, part):
    key = jax.random.fold_in(key, 11)
    key_order, key_local = jax.random.split(key)
    owner_keys = jax.random.split(key_order, N_PAIR)
    orders = jax.vmap(lambda one_key: jax.random.permutation(one_key, N_PAIR))(owner_keys)
    devices = orders[:, :2 * PB_DEV].astype(jnp.int32)
    local_block = jax.random.randint(key_local, (N_PAIR, 2 * PB_DEV), 0, BLK_DEV, jnp.int32)
    endpoints = devices * BLK_DEV + local_block
    return jnp.stack([endpoints[:, :PB_DEV], endpoints[:, PB_DEV:]], axis=-1).astype(jnp.int32)


def setup_inputs(seed: int = 0) -> dict:
    key_of = jax.random.split(jax.random.key(seed), 3)
    return {
        "spectra": draw_spectra(jax.random.fold_in(key_of[2], 71), 0),
        "pair_list": draw_pair_list(jax.random.fold_in(key_of[2], 71), 0),
    }


whiten_eps = 1e-06

def whiten(spectra):
    powers = spectra[0] * spectra[0] + spectra[1] * spectra[1]
    lead = powers.shape[:-1]
    band_power = lax.optimization_barrier(jnp.mean(powers.reshape(lead + (NF // BAND, BAND)), axis=-1))
    scales = lax.rsqrt(band_power + whiten_eps)
    banded = spectra.reshape((2,) + lead + (NF // BAND, BAND))
    return (banded * scales[None, ..., None]).reshape(spectra.shape).astype(jnp.bfloat16)

def tables(windows):
    freqs = jnp.arange(NF, dtype=jnp.int32)
    offsets = jnp.arange(NLAG, dtype=jnp.int32) - NLAG // 2
    magnitudes = jnp.abs(offsets).astype(jnp.int32)
    signs = jnp.sign(offsets).astype(jnp.float32)
    phases = jnp.mod(freqs[:, None] * magnitudes[None, :], 2 * NF)
    angles = phases.astype(jnp.float32) * (jnp.pi / NF)
    weights = jnp.where(freqs == 0, 1.0, 2.0).astype(jnp.float32) / jnp.sqrt(jnp.float32(NF * windows))
    cos_table = (weights[:, None] * jnp.cos(angles)).astype(jnp.bfloat16)
    sin_table = ((-weights)[:, None] * (signs[None, :] * jnp.sin(angles))).astype(jnp.bfloat16)
    return (cos_table, sin_table)

def crosses(source, receiver):
    highest = lax.Precision.HIGHEST
    source = source.astype(jnp.float32)
    receiver = receiver.astype(jnp.float32)
    real_part = jnp.einsum('wiaf,wibf->iabf', source[0], receiver[0], precision=highest)
    real_part = real_part + jnp.einsum('wiaf,wibf->iabf', source[1], receiver[1], precision=highest)
    imag_part = jnp.einsum('wiaf,wibf->iabf', source[1], receiver[0], precision=highest)
    imag_part = imag_part - jnp.einsum('wiaf,wibf->iabf', source[0], receiver[1], precision=highest)
    return (real_part, imag_part)

def inverse(real_part, imag_part, cos_table, sin_table):
    shape = real_part.shape
    flat_real = lax.optimization_barrier(real_part.astype(jnp.bfloat16)).astype(jnp.float32)
    flat_imag = lax.optimization_barrier(imag_part.astype(jnp.bfloat16)).astype(jnp.float32)
    flat_real = flat_real.reshape(-1, shape[-1])
    flat_imag = flat_imag.reshape(-1, shape[-1])
    lagged = jnp.dot(flat_real, cos_table, precision=lax.Precision.HIGHEST)
    lagged = lagged + jnp.dot(flat_imag, sin_table, precision=lax.Precision.HIGHEST)
    return lagged.reshape(shape[:-1] + (NLAG,))

def reference(spectra, pair_list):
    white = whiten(spectra)
    blocks = white.reshape(2, WINDOWS, N_PAIR * BLK_DEV, CH, NF)
    cos_bf, sin_bf = tables(WINDOWS)
    cos_table = lax.optimization_barrier(cos_bf).astype(jnp.float32)
    sin_table = lax.optimization_barrier(sin_bf).astype(jnp.float32)
    half_span = N_WIN // 2

    def per_owner(owner_pairs):
        source = jnp.take(blocks, owner_pairs[:, 0], axis=2)
        receiver = jnp.take(blocks, owner_pairs[:, 1], axis=2)
        real_part, imag_part = crosses(source, receiver)
        lagged = inverse(real_part, imag_part, cos_table, sin_table)
        tiled = lagged.reshape(PB_DEV, 2, SRC_TILE, half_span, RCV_TILE, NLAG)
        tiled = jnp.transpose(tiled, (0, 1, 3, 2, 4, 5))
        return tiled.reshape(PB_DEV, N_WIN, SRC_TILE, RCV_TILE, NLAG)
    stacked = lax.map(per_owner, pair_list)
    return stacked.reshape(N_PAIR * PB_DEV, N_WIN, SRC_TILE, RCV_TILE, NLAG)
```

```python
import functools

import jax
import jax.numpy as jnp
import ml_dtypes
import numpy as np
from jax import lax
from jax.experimental import pallas as pl
from jax.experimental.pallas import tpu as pltpu
from jax.sharding import PartitionSpec as P

CH = 64
BLK = 3
NF = 2048
BAND = 128
BANDS = NF // BAND
NLAG = 1024
WIN = 8
PAIR = 32
SLOTS = 2
SRC = 32
RCV = 16
PIECES = 2 * BANDS
MESH = pl.DeviceIdType.MESH

whiten_eps = 1e-06


def lag_table():
    freqs = np.arange(NF, dtype=np.int64)
    offsets = np.arange(NLAG, dtype=np.int64) - NLAG // 2
    phases = np.mod(freqs[:, None] * np.abs(offsets)[None, :], 2 * NF)
    angles = phases.astype(np.float32) * np.float32(np.pi / NF)
    weights = np.where(freqs == 0, 1.0, 2.0).astype(np.float32) / np.sqrt(np.float32(NF * WIN))
    cos_table = weights[:, None] * np.cos(angles)
    sin_table = -weights[:, None] * (np.sign(offsets).astype(np.float32)[None, :] * np.sin(angles))
    return np.concatenate([cos_table, sin_table], axis=0).astype(ml_dtypes.bfloat16)


def peer_of(me, step):
    y = lax.rem(me // 8 + step // 8, 4)
    x = lax.rem(lax.rem(me // 2, 4) + lax.rem(step // 2, 4), 4)
    core = lax.rem(lax.rem(me, 2) + lax.rem(step, 2), 2)
    return (y * 4 + x) * 2 + core


def kernel(
    list_ref, spec_ref, table_ref, out_ref,
    white, all_blocks, outgoing, mine, src_in, rcv_in, src_wide, cross, table, lagged,
    one_send, one_recv, two_send, two_recv, z_send, z_recv, local_sem, table_sem, out_sem,
):
    me = lax.axis_index("pair")
    win = lax.axis_index("win")

    barrier = pltpu.get_barrier_semaphore()

    def greet_pair(step, carry):
        pl.semaphore_signal(barrier, inc=1, device_id=(peer_of(me, step), win), device_id_type=MESH)
        return carry

    def greet_win(step, carry):
        pl.semaphore_signal(barrier, inc=1, device_id=(me, lax.rem(win + step, WIN)), device_id_type=MESH)
        return carry

    lax.fori_loop(1, PAIR, greet_pair, 0)
    lax.fori_loop(1, WIN, greet_win, 0)

    table_copy = pltpu.make_async_copy(table_ref, table, table_sem)
    table_copy.start()

    def whiten(band, carry):
        cols = pl.ds(pl.multiple_of(band * BAND, BAND), BAND)
        re = spec_ref[0, 0, :, cols]
        im = spec_ref[1, 0, :, cols]
        level = jnp.sum(re * re + im * im, axis=-1, keepdims=True) * (1.0 / BAND)
        scale = lax.rsqrt(level + whiten_eps)
        white[band] = (re * scale).astype(jnp.bfloat16).reshape(BLK, CH, BAND)
        white[BANDS + band] = (im * scale).astype(jnp.bfloat16).reshape(BLK, CH, BAND)
        return carry

    lax.fori_loop(0, BANDS, whiten, 0)

    pl.semaphore_wait(barrier, PAIR - 1 + WIN - 1)

    def send_one(step, carry):
        to = peer_of(me, step)
        pltpu.make_async_remote_copy(
            src_ref=white.at[to],
            dst_ref=all_blocks.at[pl.ds(me * BLK, BLK)],
            send_sem=one_send,
            recv_sem=one_recv,
            device_id=(to, win),
            device_id_type=MESH,
        ).start()
        return carry

    lax.fori_loop(1, PAIR, send_one, 0)
    all_blocks[pl.ds(me * BLK, BLK)] = white[me]

    most = all_blocks.at[pl.ds(0, (PAIR - 1) * BLK)]
    pltpu.make_async_copy(most, most, one_recv).wait()

    for slot in range(SLOTS):
        def send_two(step, carry):
            to = peer_of(me, step)
            for end in range(2):
                outgoing[to, slot, end] = all_blocks[list_ref[to * 4 + slot * 2 + end]]
            pltpu.make_async_remote_copy(
                src_ref=outgoing.at[to, slot],
                dst_ref=mine.at[slot, me],
                send_sem=two_send.at[slot],
                recv_sem=two_recv.at[slot],
                device_id=(to, win),
                device_id_type=MESH,
            ).start()
            return carry

        lax.fori_loop(1, PAIR, send_two, 0)
        for end in range(2):
            mine[slot, me, end] = all_blocks[list_ref[me * 4 + slot * 2 + end]]

    for slot in range(SLOTS):
        most = mine.at[slot, pl.ds(0, PAIR - 1)]
        pltpu.make_async_copy(most, most, two_recv.at[slot]).wait()

        def views(to):
            src = mine.at[slot, :, 0, pl.ds(pl.multiple_of(to // 4 * SRC, SRC), SRC)]
            rcv = mine.at[slot, :, 1, pl.ds(pl.multiple_of(lax.rem(to, 4) * RCV, RCV), RCV)]
            return src, rcv

        def send_z(step, carry):
            to = lax.rem(win + step, WIN)
            src, rcv = views(to)
            for part, (view, dst) in enumerate(((src, src_in), (rcv, rcv_in))):
                pltpu.make_async_remote_copy(
                    src_ref=view,
                    dst_ref=dst.at[slot, win],
                    send_sem=z_send.at[slot, part],
                    recv_sem=z_recv.at[slot, part],
                    device_id=(me, to),
                    device_id_type=MESH,
                ).start()
            return carry

        lax.fori_loop(1, WIN, send_z, 0)
        src, rcv = views(win)
        pltpu.make_async_copy(src, src_in.at[slot, win], local_sem.at[slot, 0]).start()
        pltpu.make_async_copy(rcv, rcv_in.at[slot, win], local_sem.at[slot, 1]).start()

    table_copy.wait()

    for slot in range(SLOTS):
        src, rcv = src_in.at[slot], rcv_in.at[slot]
        for part, ref in enumerate((src, rcv)):
            most = ref.at[pl.ds(0, WIN - 1)]
            pltpu.make_async_copy(most, most, z_recv.at[slot, part]).wait()
            pltpu.make_async_copy(ref.at[0], ref.at[0], local_sem.at[slot, part]).wait()

        def one_band(band, carry):
            receivers = []
            for w in range(WIN):
                for part in range(2):
                    src_wide[part, w] = src[w, part * BANDS + band].astype(jnp.float32)
                    receivers.append(rcv[w, part * BANDS + band].astype(jnp.float32))

            def one_source(a, inner):
                re = jnp.zeros((RCV, BAND), jnp.float32)
                im = jnp.zeros((RCV, BAND), jnp.float32)
                for w in range(WIN):
                    s_re = jnp.broadcast_to(src_wide[0, w, pl.ds(a, 1), :], (RCV, BAND))
                    s_im = jnp.broadcast_to(src_wide[1, w, pl.ds(a, 1), :], (RCV, BAND))
                    r_re, r_im = receivers[2 * w], receivers[2 * w + 1]
                    re = re + s_re * r_re + s_im * r_im
                    im = im + s_im * r_re - s_re * r_im
                rows = pl.ds(pl.multiple_of(a * RCV, RCV), RCV)
                cross[rows, pl.ds(pl.multiple_of(band * BAND, BAND), BAND)] = re.astype(jnp.bfloat16)
                cross[rows, pl.ds(pl.multiple_of(NF + band * BAND, BAND), BAND)] = im.astype(jnp.bfloat16)
                return inner

            lax.fori_loop(0, SRC, one_source, 0)
            return carry

        lax.fori_loop(0, BANDS, one_band, 0)

        def one_tile(tile, carry):
            cols = pl.ds(pl.multiple_of(tile * 256, 256), 256)
            lagged[slot, :, cols] = jnp.dot(cross[...], table[:, cols], preferred_element_type=jnp.float32)
            return carry

        lax.fori_loop(0, NLAG // 256, one_tile, 0)
        pltpu.make_async_copy(lagged.at[slot], out_ref.at[slot], out_sem.at[slot]).start()

    sent = white.at[pl.ds(0, PAIR - 1)]
    pltpu.make_async_copy(sent, sent, one_send).wait()
    for slot in range(SLOTS):
        sent = outgoing.at[pl.ds(0, PAIR - 1), slot]
        pltpu.make_async_copy(sent, sent, two_send.at[slot]).wait()
        for part, ref in enumerate((src_in, rcv_in)):
            sent = ref.at[slot, pl.ds(0, WIN - 1)]
            pltpu.make_async_copy(sent, sent, z_send.at[slot, part]).wait()
        pltpu.make_async_copy(lagged.at[slot], out_ref.at[slot], out_sem.at[slot]).wait()


def body(spectra, pair_list):
    table = jnp.asarray(lag_table())
    rows = SRC * RCV
    bf16 = jnp.bfloat16
    out = pl.pallas_call(
        kernel,
        out_shape=jax.ShapeDtypeStruct((SLOTS, rows, NLAG), jnp.float32),
        in_specs=[
            pl.BlockSpec(memory_space=pltpu.SMEM),
            pl.BlockSpec(memory_space=pltpu.VMEM),
            pl.BlockSpec(memory_space=pl.ANY),
        ],
        out_specs=pl.BlockSpec(memory_space=pl.ANY),
        scratch_shapes=[
            pltpu.VMEM((PIECES, BLK, CH, BAND), bf16),
            pltpu.VMEM((PAIR * BLK, CH, BAND), bf16),
            pltpu.VMEM((PAIR, SLOTS, 2, CH, BAND), bf16),
            pltpu.VMEM((SLOTS, PIECES, 2, CH, BAND), bf16),
            pltpu.VMEM((SLOTS, WIN, PIECES, SRC, BAND), bf16),
            pltpu.VMEM((SLOTS, WIN, PIECES, RCV, BAND), bf16),
            pltpu.VMEM((2, WIN, SRC, BAND), jnp.float32),
            pltpu.VMEM((rows, 2 * NF), bf16),
            pltpu.VMEM((2 * NF, NLAG), bf16),
            pltpu.VMEM((SLOTS, rows, NLAG), jnp.float32),
            pltpu.SemaphoreType.DMA,
            pltpu.SemaphoreType.DMA,
            pltpu.SemaphoreType.DMA((SLOTS,)),
            pltpu.SemaphoreType.DMA((SLOTS,)),
            pltpu.SemaphoreType.DMA((SLOTS, 2)),
            pltpu.SemaphoreType.DMA((SLOTS, 2)),
            pltpu.SemaphoreType.DMA((SLOTS, 2)),
            pltpu.SemaphoreType.DMA,
            pltpu.SemaphoreType.DMA((SLOTS,)),
        ],
        compiler_params=pltpu.CompilerParams(
            collective_id=0, has_side_effects=True, vmem_limit_bytes=48 * 1024 * 1024
        ),
    )(pair_list.reshape(-1), spectra, table)
    return out.reshape(SLOTS, 1, SRC, RCV, NLAG)


def solution(mesh):
    in_specs = (P(None, "win", "pair", None), P())
    out_specs = P("pair", "win", None, None, None)
    return jax.shard_map(body, mesh=mesh, in_specs=in_specs, out_specs=out_specs, check_vma=False)
```

```python
import functools

import jax
import jax.numpy as jnp
import ml_dtypes
import numpy as np
from jax import lax
from jax.experimental import pallas as pl
from jax.experimental.pallas import tpu as pltpu
from jax.sharding import PartitionSpec as P

CH = 64
BLK = 3
NF = 2048
BAND = 128
BANDS = NF // BAND
NLAG = 1024
WIN = 8
PAIR = 32
SLOTS = 2
SRC = 32
RCV = 16
PIECES = 2 * BANDS
GROUP = 16
STAGES = [(0, 1), (0, 0), (1, 1), (1, 0)]
MESH = pl.DeviceIdType.MESH

whiten_eps = 1e-06


def lag_table():
    freqs = np.arange(NF, dtype=np.int64)
    offsets = np.arange(NLAG, dtype=np.int64) - NLAG // 2
    phases = np.mod(freqs[:, None] * np.abs(offsets)[None, :], 2 * NF)
    angles = phases.astype(np.float32) * np.float32(np.pi / NF)
    weights = np.where(freqs == 0, 1.0, 2.0).astype(np.float32) / np.sqrt(np.float32(NF * WIN))
    cos_table = weights[:, None] * np.cos(angles)
    sin_table = -weights[:, None] * (np.sign(offsets).astype(np.float32)[None, :] * np.sin(angles))
    return np.concatenate([cos_table, sin_table], axis=0).astype(ml_dtypes.bfloat16)


def peer_of(me, step):
    y = lax.rem(me // 8 + step // 8, 4)
    x = lax.rem(lax.rem(me // 2, 4) + lax.rem(step // 2, 4), 4)
    core = lax.rem(lax.rem(me, 2) + lax.rem(step, 2), 2)
    return (y * 4 + x) * 2 + core


def job_of(device, win):
    x, core = lax.rem(device // 2, 4), lax.rem(device, 2)
    return x // 2, lax.rem(lax.rem(x, 2) + 2 * core + win // 2, 4)


def kernel(
    list_ref, spec_ref, table_ref, out_ref,
    spec, white, blocks_0, blocks_1, outgoing, plane_in, job_in, src_wide, cross, table, result,
    spec_sem, table_sem, one_send, one_recv, z_send, z_recv, two_send, two_recv, back_send, back_recv,
):
    me = lax.axis_index("pair")
    win = lax.axis_index("win")
    row, column = me // 8, lax.rem(me, 8)

    spec_copy = pltpu.make_async_copy(spec_ref, spec, spec_sem)
    spec_copy.start()
    table_copy = pltpu.make_async_copy(table_ref, table, table_sem)
    table_copy.start()

    slot, quad = job_of(me, win)
    owner = row * 8 + win
    tiles = [quad * 2 + t for t in range(2)]
    own = [(owner == me) & (tile == win) for tile in tiles]
    shift = lax.rem(win // 2 - column // 2 + 4, 4)
    makers = [row * 8 + (2 * i + lax.rem(shift, 2)) * 2 + shift // 2 for i in range(SLOTS)]

    barrier = pltpu.get_barrier_semaphore()

    def greet(pair, plane):
        pl.semaphore_signal(barrier, inc=1, device_id=(pair, plane), device_id_type=MESH)

    def greet_pair(step, carry):
        greet(peer_of(me, step), win)
        return carry

    def greet_win(step, carry):
        greet(me, lax.rem(win + step, WIN))
        return carry

    lax.fori_loop(1, PAIR, greet_pair, 0)
    lax.fori_loop(1, WIN, greet_win, 0)
    count = PAIR - 1 + WIN - 1
    for t in range(2):
        here = own[t]

        @pl.when(jnp.logical_not(here))
        def _():
            greet(owner, tiles[t])

        count = count + jnp.where(here, 0, 1)
    for i in range(SLOTS):
        here = (makers[i] == me) & (column == win)

        @pl.when(jnp.logical_not(here))
        def _():
            greet(makers[i], column)

        count = count + jnp.where(here, 0, 1)

    all_blocks = (blocks_0, blocks_1)

    spec_copy.wait()

    def whiten(band, carry):
        cols = pl.ds(pl.multiple_of(band * BAND, BAND), BAND)
        re = spec[0, 0, :, cols]
        im = spec[1, 0, :, cols]
        level = jnp.sum(re * re + im * im, axis=-1, keepdims=True) * (1.0 / BAND)
        scale = lax.rsqrt(level + whiten_eps)
        for part, value in enumerate((re, im)):
            piece = (value * scale).astype(jnp.bfloat16).reshape(BLK, 2, 2, GROUP, BAND)
            for k in range(2):
                white[k, part * BANDS + band] = piece[:, :, k]
        return carry

    lax.fori_loop(0, BANDS, whiten, 0)

    pl.semaphore_wait(barrier, count)

    for k in range(2):
        def send_one(step, carry):
            to = peer_of(me, step)
            pltpu.make_async_remote_copy(
                src_ref=white.at[k, to],
                dst_ref=all_blocks[k].at[pl.ds(me * BLK, BLK)],
                send_sem=one_send.at[k],
                recv_sem=one_recv.at[k],
                device_id=(to, win),
                device_id_type=MESH,
            ).start()
            return carry

        lax.fori_loop(1, PAIR, send_one, 0)
        all_blocks[k][pl.ds(me * BLK, BLK)] = white[k, me]

    for stage, (k, role) in enumerate(STAGES):
        if stage % 2 == 0:
            most = all_blocks[k].at[pl.ds(0, (PAIR - 1) * BLK)]
            pltpu.make_async_copy(most, most, one_recv.at[k]).wait()

        def pick(plane):
            return [
                (o, i, all_blocks[k][list_ref[(o * 8 + plane) * 4 + i * 2 + role]])
                for o in range(4) for i in range(SLOTS)
            ]

        def send_z(step, carry):
            to = lax.rem(win + step, WIN)
            for o, i, block in pick(to):
                outgoing[stage, to, o, i] = block
            pltpu.make_async_remote_copy(
                src_ref=outgoing.at[stage, to],
                dst_ref=plane_in.at[stage, win],
                send_sem=z_send.at[stage],
                recv_sem=z_recv.at[stage],
                device_id=(me, to),
                device_id_type=MESH,
            ).start()
            return carry

        lax.fori_loop(1, WIN, send_z, 0)
        for o, i, block in pick(win):
            plane_in[stage, win, o, i] = block

    def spread(stage):
        k, role = STAGES[stage]
        most = plane_in.at[stage, pl.ds(0, WIN - 1)]
        pltpu.make_async_copy(most, most, z_recv.at[stage]).wait()

        def view(to):
            i, pair_of_tiles = job_of(to, win)
            half = pair_of_tiles // 2 if role == 0 else lax.rem(pair_of_tiles, 2)
            return plane_in.at[stage, :, to // 8, i, half]

        def send_two(step, carry):
            to = peer_of(me, step)
            pltpu.make_async_remote_copy(
                src_ref=view(to),
                dst_ref=job_in.at[stage, me],
                send_sem=two_send.at[stage],
                recv_sem=two_recv.at[stage],
                device_id=(to, win),
                device_id_type=MESH,
            ).start()
            return carry

        lax.fori_loop(1, PAIR, send_two, 0)
        job_in[stage, me] = view(me)[...]

    def arrived(stage):
        most = job_in.at[stage, pl.ds(0, PAIR - 1)]
        pltpu.make_async_copy(most, most, two_recv.at[stage]).wait()

    def work(half, t):
        src, rcv = job_in.at[STAGES.index((half, 0))], job_in.at[STAGES.index((t, 1))]
        unit = half * 2 + t

        def one_band(band, carry):
            receivers = []
            for w in range(WIN):
                for part in range(2):
                    src_wide[part, w] = src[part * BANDS + band, w].astype(jnp.float32)
                    receivers.append(rcv[part * BANDS + band, w].astype(jnp.float32))

            def one_source(a, inner):
                re = jnp.zeros((RCV, BAND), jnp.float32)
                im = jnp.zeros((RCV, BAND), jnp.float32)
                for w in range(WIN):
                    s_re = jnp.broadcast_to(src_wide[0, w, pl.ds(a, 1), :], (RCV, BAND))
                    s_im = jnp.broadcast_to(src_wide[1, w, pl.ds(a, 1), :], (RCV, BAND))
                    r_re, r_im = receivers[2 * w], receivers[2 * w + 1]
                    re = re + s_re * r_re + s_im * r_im
                    im = im + s_im * r_re - s_re * r_im
                rows = pl.ds(pl.multiple_of(a * RCV, RCV), RCV)
                cross[rows, pl.ds(pl.multiple_of(band * BAND, BAND), BAND)] = re.astype(jnp.bfloat16)
                cross[rows, pl.ds(pl.multiple_of(NF + band * BAND, BAND), BAND)] = im.astype(jnp.bfloat16)
                return inner

            lax.fori_loop(0, GROUP, one_source, 0)
            return carry

        lax.fori_loop(0, BANDS, one_band, 0)

        def one_tile(tile, carry):
            cols = pl.ds(pl.multiple_of(tile * 256, 256), 256)
            lags = jnp.dot(cross[...], table[:, cols], preferred_element_type=jnp.float32)
            result[unit, :, cols] = lags.astype(jnp.bfloat16)
            return carry

        lax.fori_loop(0, NLAG // 256, one_tile, 0)

        @pl.when(own[t])
        def _():
            pltpu.make_async_copy(result.at[unit], out_ref.at[slot, half], back_recv.at[slot, half]).start()

        @pl.when(jnp.logical_not(own[t]))
        def _():
            pltpu.make_async_remote_copy(
                src_ref=result.at[unit],
                dst_ref=out_ref.at[slot, half],
                send_sem=back_send.at[unit],
                recv_sem=back_recv.at[slot, half],
                device_id=(owner, tiles[t]),
                device_id_type=MESH,
            ).start()

    spread(0)
    spread(1)
    spread(2)
    table_copy.wait()
    arrived(0)
    arrived(1)
    work(0, 0)
    spread(3)
    arrived(2)
    work(0, 1)
    arrived(3)
    work(1, 0)
    work(1, 1)

    for k in range(2):
        sent = white.at[k, pl.ds(0, PAIR - 1)]
        pltpu.make_async_copy(sent, sent, one_send.at[k]).wait()
    for stage in range(4):
        sent = outgoing.at[stage, pl.ds(0, WIN - 1)]
        pltpu.make_async_copy(sent, sent, z_send.at[stage]).wait()
        sent = job_in.at[stage, pl.ds(0, PAIR - 1)]
        pltpu.make_async_copy(sent, sent, two_send.at[stage]).wait()
    for half in range(2):
        for t in range(2):
            sent = result.at[half * 2 + t]

            @pl.when(jnp.logical_not(own[t]))
            def _():
                pltpu.make_async_copy(sent, sent, back_send.at[half * 2 + t]).wait()

        for i in range(SLOTS):
            tile = out_ref.at[i, half]
            pltpu.make_async_copy(tile, tile, back_recv.at[i, half]).wait()


def body(spectra, pair_list):
    table = jnp.asarray(lag_table())
    rows = GROUP * RCV
    bf16 = jnp.bfloat16
    dma = pltpu.SemaphoreType.DMA
    out = pl.pallas_call(
        kernel,
        out_shape=jax.ShapeDtypeStruct((SLOTS, 2, rows, NLAG), bf16),
        in_specs=[
            pl.BlockSpec(memory_space=pltpu.SMEM),
            pl.BlockSpec(memory_space=pl.ANY),
            pl.BlockSpec(memory_space=pl.ANY),
        ],
        out_specs=pl.BlockSpec(memory_space=pl.ANY),
        scratch_shapes=[
            pltpu.VMEM((2, 1, BLK * CH, NF), jnp.float32),
            pltpu.VMEM((2, PIECES, BLK, 2, GROUP, BAND), bf16),
            pltpu.VMEM((PAIR * BLK, 2, GROUP, BAND), bf16),
            pltpu.VMEM((PAIR * BLK, 2, GROUP, BAND), bf16),
            pltpu.VMEM((4, WIN, 4, SLOTS, 2, GROUP, BAND), bf16),
            pltpu.VMEM((4, WIN, 4, SLOTS, 2, GROUP, BAND), bf16),
            pltpu.VMEM((4, PIECES, WIN, GROUP, BAND), bf16),
            pltpu.VMEM((2, WIN, GROUP, BAND), jnp.float32),
            pltpu.VMEM((rows, 2 * NF), bf16),
            pltpu.VMEM((2 * NF, NLAG), bf16),
            pltpu.VMEM((4, rows, NLAG), bf16),
            dma, dma,
            dma((2,)), dma((2,)),
            dma((4,)), dma((4,)),
            dma((4,)), dma((4,)),
            dma((4,)), dma((SLOTS, 2)),
        ],
        compiler_params=pltpu.CompilerParams(
            collective_id=0, has_side_effects=True, vmem_limit_bytes=48 * 1024 * 1024
        ),
    )(pair_list.reshape(-1), spectra, table)
    return out.astype(jnp.float32).reshape(SLOTS, 1, SRC, RCV, NLAG)


def solution(mesh):
    in_specs = (P(None, "win", "pair", None), P())
    out_specs = P("pair", "win", None, None, None)
    return jax.shard_map(body, mesh=mesh, in_specs=in_specs, out_specs=out_specs, check_vma=False)
```

```python
import functools

import jax
import jax.numpy as jnp
import ml_dtypes
import numpy as np
from jax import lax
from jax.experimental import pallas as pl
from jax.experimental.pallas import tpu as pltpu
from jax.sharding import PartitionSpec as P

CH = 64
BLK = 3
NF = 2048
BAND = 128
BANDS = NF // BAND
NLAG = 1024
WIN = 8
PAIR = 32
SLOTS = 2
SRC = 32
RCV = 16
PIECES = 2 * BANDS
GROUP = 16
PART = 8
STAGES = [(0, 1), (0, 0), (1, 1), (1, 0)]
MESH = pl.DeviceIdType.MESH

whiten_eps = 1e-06


def lag_table():
    freqs = np.arange(NF, dtype=np.int64)
    offsets = np.arange(NLAG, dtype=np.int64) - NLAG // 2
    phases = np.mod(freqs[:, None] * np.abs(offsets)[None, :], 2 * NF)
    angles = phases.astype(np.float32) * np.float32(np.pi / NF)
    weights = np.where(freqs == 0, 1.0, 2.0).astype(np.float32) / np.sqrt(np.float32(NF * WIN))
    cos_table = weights[:, None] * np.cos(angles)
    sin_table = -weights[:, None] * (np.sign(offsets).astype(np.float32)[None, :] * np.sin(angles))
    return np.concatenate([cos_table, sin_table], axis=0).astype(ml_dtypes.bfloat16)


def peer_of(me, step):
    y = lax.rem(me // 8 + step // 8, 4)
    x = lax.rem(lax.rem(me // 2, 4) + lax.rem(step // 2, 4), 4)
    core = lax.rem(lax.rem(me, 2) + lax.rem(step, 2), 2)
    return (y * 4 + x) * 2 + core


def job_of(device, win):
    x, core = lax.rem(device // 2, 4), lax.rem(device, 2)
    return core, lax.rem(x + 2 * lax.rem(win + core, 2) + win // 2, 4)


def kernel(
    list_ref, spec_ref, table_ref, out_ref,
    spec, white, blocks_0, blocks_1, outgoing, plane_in, src_in, rcv_in, src_wide, cross, table, result,
    spec_sem, table_sem, one_send, one_recv, z_send, z_recv, two_send, two_recv, back_send, back_recv,
):
    me = lax.axis_index("pair")
    win = lax.axis_index("win")
    row, column = me // 8, lax.rem(me, 8)
    chip, core = me // 2, lax.rem(me, 2)

    spec_copy = pltpu.make_async_copy(spec_ref, spec, spec_sem)
    spec_copy.start()
    table_copy = pltpu.make_async_copy(table_ref, table, table_sem)
    table_copy.start()

    slot, quad = job_of(me, win)
    owner = row * 8 + win

    def is_own(t):
        return (owner == me) & (quad * 2 + t == win)

    shift = win // 2 - column // 2 + 4
    makers = [row * 8 + lax.rem(shift + 2 * lax.rem(column + i, 2), 4) * 2 + i for i in range(SLOTS)]

    barrier = pltpu.get_barrier_semaphore()

    def greet(pair, plane):
        pl.semaphore_signal(barrier, inc=1, device_id=(pair, plane), device_id_type=MESH)

    def greet_pair(step, carry):
        greet(peer_of(me, step), win)
        return carry

    def greet_win(step, carry):
        greet(me, lax.rem(win + step, WIN))
        return carry

    lax.fori_loop(1, PAIR, greet_pair, 0)
    lax.fori_loop(1, WIN, greet_win, 0)
    count = PAIR - 1 + WIN - 1
    for t in range(2):
        here = is_own(t)

        @pl.when(jnp.logical_not(here))
        def _():
            greet(owner, quad * 2 + t)

        count = count + jnp.where(here, 0, 1)
    for i in range(SLOTS):
        here = (makers[i] == me) & (column == win)

        @pl.when(jnp.logical_not(here))
        def _():
            greet(makers[i], column)

        count = count + jnp.where(here, 0, 1)

    all_blocks = (blocks_0, blocks_1)

    spec_copy.wait()

    def whiten(band, carry):
        cols = pl.ds(pl.multiple_of(band * BAND, BAND), BAND)
        re = spec[0, 0, :, cols]
        im = spec[1, 0, :, cols]
        level = jnp.sum(re * re + im * im, axis=-1, keepdims=True) * (1.0 / BAND)
        scale = lax.rsqrt(level + whiten_eps)
        for part, value in enumerate((re, im)):
            piece = (value * scale).astype(jnp.bfloat16).reshape(BLK, 2, 2, GROUP, BAND)
            for k in range(2):
                white[k, part * BANDS + band] = piece[:, :, k]
        return carry

    lax.fori_loop(0, BANDS, whiten, 0)

    pl.semaphore_wait(barrier, count)

    def one_copy(k, step):
        to = peer_of(me, step)
        return pltpu.make_async_remote_copy(
            src_ref=white.at[k, to],
            dst_ref=all_blocks[k].at[pl.ds(me * BLK, BLK)],
            send_sem=one_send.at[k, step],
            recv_sem=one_recv.at[k],
            device_id=(to, win),
            device_id_type=MESH,
        )

    def scatter(k):
        def send_one(step, carry):
            if k:
                one_copy(k - 1, step).wait_send()
            one_copy(k, step).start()
            return carry

        lax.fori_loop(1, PAIR, send_one, 0)
        all_blocks[k][pl.ds(me * BLK, BLK)] = white[k, me]

    def scatter_arrived(k):
        most = all_blocks[k].at[pl.ds(0, (PAIR - 1) * BLK)]
        pltpu.make_async_copy(most, most, one_recv.at[k]).wait()

    def pick(stage):
        i = stage // 4
        k, role = STAGES[stage % 4]

        def pick_for(step, carry):
            to = lax.rem(win + step, WIN)
            for o in range(4):
                outgoing[stage, to, o] = all_blocks[k][list_ref[(o * 8 + to) * 4 + i * 2 + role]]
            return carry

        lax.fori_loop(1, WIN, pick_for, 0)
        for o in range(4):
            plane_in[stage, win, o] = all_blocks[k][list_ref[(o * 8 + win) * 4 + i * 2 + role]]

    def z_copy(stage, step):
        to = lax.rem(win + step, WIN)
        return pltpu.make_async_remote_copy(
            src_ref=outgoing.at[stage, to],
            dst_ref=plane_in.at[stage, win],
            send_sem=z_send.at[stage, step],
            recv_sem=z_recv.at[stage],
            device_id=(me, to),
            device_id_type=MESH,
        )

    def send_planes(stage):
        def send_z(step, carry):
            if stage:
                z_copy(stage - 1, step).wait_send()
            z_copy(stage, step).start()
            return carry

        lax.fori_loop(1, WIN, send_z, 0)

    def spread(stage):
        i = stage // 4
        k, role = STAGES[stage % 4]
        most = plane_in.at[stage, pl.ds(0, WIN - 1)]
        pltpu.make_async_copy(most, most, z_recv.at[stage]).wait()
        dst = (rcv_in if role else src_in).at[k, me]

        def view(to):
            quad_there = job_of(to, win)[1]
            half = lax.rem(quad_there, 2) if role else quad_there // 2
            return plane_in.at[stage, :, to // 8, half]

        def send_two(step, carry):
            to = peer_of(me, step * 2 + lax.rem(core + i, 2))
            pltpu.make_async_remote_copy(
                src_ref=view(to),
                dst_ref=dst,
                send_sem=two_send.at[stage],
                recv_sem=two_recv.at[stage % 4],
                device_id=(to, win),
                device_id_type=MESH,
            ).start()
            return carry

        @pl.when(core == i)
        def _():
            dst[...] = view(me)[...]

        lax.fori_loop(jnp.where(core == i, 1, 0), PAIR // 2, send_two, 0)

    def arrived(j):
        k, role = STAGES[j]
        most = (rcv_in if role else src_in).at[k, pl.ds(0, PAIR - 1)]
        pltpu.make_async_copy(most, most, two_recv.at[j]).wait()

    def work(unit):
        half, t = unit // 2, unit % 2
        src, rcv = src_in.at[half], rcv_in.at[t]
        here = is_own(t)

        def one_part(e, carry):
            def one_band(band, inner):
                receivers = []
                for w in range(WIN):
                    s_re = src[band, w].astype(jnp.float32)
                    s_im = src[BANDS + band, w].astype(jnp.float32)
                    for n, value in enumerate((s_re, s_im, s_re + s_im)):
                        src_wide[n, w] = value
                    r_re = rcv[band, w].astype(jnp.float32)
                    r_im = rcv[BANDS + band, w].astype(jnp.float32)
                    receivers.append((r_re, r_re + r_im, r_re - r_im))

                for a in range(PART):
                    both = left = right = jnp.zeros((RCV, BAND), jnp.float32)
                    for w in range(WIN):
                        s_re, s_im, s_sum = (
                            jnp.broadcast_to(src_wide[n, w, pl.ds(e * PART + a, 1), :], (RCV, BAND)) for n in range(3)
                        )
                        r_re, r_sum, r_diff = receivers[w]
                        both = both + s_sum * r_re
                        left = left + s_re * r_sum
                        right = right + s_im * r_diff
                    rows = pl.ds(a * RCV, RCV)
                    cols = pl.multiple_of(band * BAND, BAND)
                    cross[rows, pl.ds(cols, BAND)] = (both - right).astype(jnp.bfloat16)
                    cross[rows, pl.ds(NF + cols, BAND)] = (both - left).astype(jnp.bfloat16)
                return inner

            lax.fori_loop(0, BANDS, one_band, 0)
            rows = pl.ds(pl.multiple_of(e * PART * RCV, PART * RCV), PART * RCV)

            def one_tile(tile, inner):
                cols = pl.ds(pl.multiple_of(tile * 512, 512), 512)
                lags = jnp.dot(cross[...], table[:, cols], preferred_element_type=jnp.float32)
                result[unit, rows, cols] = lags.astype(jnp.bfloat16)
                return inner

            lax.fori_loop(0, NLAG // 512, one_tile, 0)

            @pl.when(here)
            def _():
                pltpu.make_async_copy(
                    result.at[unit, rows], out_ref.at[slot, half, rows], back_recv.at[slot, half, e]
                ).start()

            @pl.when(jnp.logical_not(here))
            def _():
                pltpu.make_async_remote_copy(
                    src_ref=result.at[unit, rows],
                    dst_ref=out_ref.at[slot, half, rows],
                    send_sem=back_send.at[unit, e],
                    recv_sem=back_recv.at[slot, half, e],
                    device_id=(owner, quad * 2 + t),
                    device_id_type=MESH,
                ).start()

            return carry

        lax.fori_loop(0, GROUP // PART, one_part, 0)

    def work_after(i, unit, *stages):
        @pl.when(core == i)
        def _():
            for j in stages:
                arrived(j)
            work(unit)

    scatter(0)
    scatter(1)
    scatter_arrived(0)
    pick(0)
    send_planes(0)
    pick(1)
    send_planes(1)
    spread(0)
    scatter_arrived(1)
    pick(2)
    send_planes(2)
    pick(3)
    spread(1)
    send_planes(3)
    pick(4)
    spread(2)
    send_planes(4)
    pick(5)
    spread(3)
    send_planes(5)
    pick(6)
    pick(7)
    table_copy.wait()
    spread(4)
    send_planes(6)
    work_after(0, 0, 0, 1)
    spread(5)
    send_planes(7)
    work_after(0, 1, 2)
    spread(6)
    work_after(0, 2, 3)
    spread(7)
    work_after(0, 3)
    work_after(1, 0, 0, 1)
    work_after(1, 1, 2)
    work_after(1, 2, 3)
    work_after(1, 3)

    def last_sent(step, carry):
        one_copy(1, step).wait_send()
        return carry

    lax.fori_loop(1, PAIR, last_sent, 0)
    for step in range(1, WIN):
        z_copy(7, step).wait_send()
    for stage in range(8):
        for i in range(2):
            @pl.when(lax.rem(core + i, 2) == stage // 4)
            def _():
                sent = src_in.at[0, pl.ds(0, PAIR // 2 - 1 + i)]
                pltpu.make_async_copy(sent, sent, two_send.at[stage]).wait()

    for half in range(2):
        for e in range(GROUP // PART):
            rows = pl.ds(e * PART * RCV, PART * RCV)
            for t in range(2):
                sent = result.at[half * 2 + t, rows]

                @pl.when(jnp.logical_not(is_own(t)))
                def _():
                    pltpu.make_async_copy(sent, sent, back_send.at[half * 2 + t, e]).wait()

            for i in range(SLOTS):
                tile = out_ref.at[i, half, rows]
                pltpu.make_async_copy(tile, tile, back_recv.at[i, half, e]).wait()


def body(spectra, pair_list):
    table = jnp.asarray(lag_table())
    rows = GROUP * RCV
    bf16 = jnp.bfloat16
    dma = pltpu.SemaphoreType.DMA
    out = pl.pallas_call(
        kernel,
        out_shape=jax.ShapeDtypeStruct((SLOTS, 2, rows, NLAG), bf16),
        in_specs=[
            pl.BlockSpec(memory_space=pltpu.SMEM),
            pl.BlockSpec(memory_space=pl.ANY),
            pl.BlockSpec(memory_space=pl.ANY),
        ],
        out_specs=pl.BlockSpec(memory_space=pl.ANY),
        scratch_shapes=[
            pltpu.VMEM((2, 1, BLK * CH, NF), jnp.float32),
            pltpu.VMEM((2, PIECES, BLK, 2, GROUP, BAND), bf16),
            pltpu.VMEM((PAIR * BLK, 2, GROUP, BAND), bf16),
            pltpu.VMEM((PAIR * BLK, 2, GROUP, BAND), bf16),
            pltpu.VMEM((8, WIN, 4, 2, GROUP, BAND), bf16),
            pltpu.VMEM((8, WIN, 4, 2, GROUP, BAND), bf16),
            pltpu.VMEM((2, PIECES, WIN, GROUP, BAND), bf16),
            pltpu.VMEM((2, PIECES, WIN, GROUP, BAND), bf16),
            pltpu.VMEM((3, WIN, GROUP, BAND), jnp.float32),
            pltpu.VMEM((PART * RCV, 2 * NF), bf16),
            pltpu.VMEM((2 * NF, NLAG), bf16),
            pltpu.VMEM((4, rows, NLAG), bf16),
            dma, dma,
            dma((2, PAIR)), dma((2,)),
            dma((8, WIN)), dma((8,)),
            dma((8,)), dma((4,)),
            dma((4, GROUP // PART)), dma((SLOTS, 2, GROUP // PART)),
        ],
        compiler_params=pltpu.CompilerParams(
            collective_id=0, has_side_effects=True, vmem_limit_bytes=60 * 1024 * 1024
        ),
    )(pair_list.reshape(-1), spectra, table)
    return out.astype(jnp.float32).reshape(SLOTS, 1, SRC, RCV, NLAG)


def solution(mesh):
    in_specs = (P(None, "win", "pair", None), P())
    out_specs = P("pair", "win", None, None, None)
    return jax.shard_map(body, mesh=mesh, in_specs=in_specs, out_specs=out_specs, check_vma=False)
```

```python
import functools

import jax
import jax.numpy as jnp
import ml_dtypes
import numpy as np
from jax import lax
from jax.experimental import pallas as pl
from jax.experimental.pallas import tpu as pltpu
from jax.sharding import PartitionSpec as P

CH = 64
BLK = 3
NF = 2048
BAND = 128
BANDS = NF // BAND
NLAG = 1024
WIN = 8
PAIR = 32
SLOTS = 2
SRC = 32
RCV = 16
PIECES = 2 * BANDS
GROUP = 16
PART = 8
STAGES = [(0, 1), (0, 0), (1, 1), (1, 0)]
SENDS = [(0, (0,)), (1, (0,)), (0, (1,)), (1, (1,))] + [(stage, (0, 1)) for stage in range(2, 8)]
MESH = pl.DeviceIdType.MESH

whiten_eps = 1e-06


def lag_table():
    freqs = np.arange(NF, dtype=np.int64)
    offsets = np.arange(NLAG, dtype=np.int64) - NLAG // 2
    phases = np.mod(freqs[:, None] * np.abs(offsets)[None, :], 2 * NF)
    angles = phases.astype(np.float32) * np.float32(np.pi / NF)
    weights = np.where(freqs == 0, 1.0, 2.0).astype(np.float32) / np.sqrt(np.float32(NF * WIN))
    cos_table = weights[:, None] * np.cos(angles)
    sin_table = -weights[:, None] * (np.sign(offsets).astype(np.float32)[None, :] * np.sin(angles))
    return np.concatenate([cos_table, sin_table], axis=0).astype(ml_dtypes.bfloat16)


def peer_of(me, step):
    y = lax.rem(me // 8 + step // 8, 4)
    x = lax.rem(lax.rem(me // 2, 4) + lax.rem(step // 2, 4), 4)
    core = lax.rem(lax.rem(me, 2) + lax.rem(step, 2), 2)
    return (y * 4 + x) * 2 + core


def job_of(device, win):
    x, core = lax.rem(device // 2, 4), lax.rem(device, 2)
    return core, lax.rem(x + 2 * lax.rem(win + core, 2) + win // 2, 4)


def kernel(
    list_ref, spec_ref, table_ref, out_ref,
    spec, white, blocks_0, blocks_1, blocks_2, blocks_3, outgoing, plane_in, src_in, rcv_in, src_wide, cross, table, result,
    spec_sem, table_sem, one_send, one_recv, z_send, z_recv, two_send, two_recv, back_send, back_recv,
):
    me = lax.axis_index("pair")
    win = lax.axis_index("win")
    row, column = me // 8, lax.rem(me, 8)
    chip, core = me // 2, lax.rem(me, 2)

    spec_copy = pltpu.make_async_copy(spec_ref, spec, spec_sem)
    spec_copy.start()
    table_copy = pltpu.make_async_copy(table_ref, table, table_sem)
    table_copy.start()

    slot, quad = job_of(me, win)
    owner = row * 8 + win

    def is_own(t):
        return (owner == me) & (quad * 2 + t == win)

    shift = win // 2 - column // 2 + 4
    makers = [row * 8 + lax.rem(shift + 2 * lax.rem(column + i, 2), 4) * 2 + i for i in range(SLOTS)]

    barrier = pltpu.get_barrier_semaphore()

    def greet(pair, plane):
        pl.semaphore_signal(barrier, inc=1, device_id=(pair, plane), device_id_type=MESH)

    def greet_pair(step, carry):
        greet(peer_of(me, step), win)
        return carry

    def greet_win(step, carry):
        greet(me, lax.rem(win + step, WIN))
        return carry

    lax.fori_loop(1, PAIR, greet_pair, 0)
    lax.fori_loop(1, WIN, greet_win, 0)
    count = PAIR - 1 + WIN - 1
    for t in range(2):
        here = is_own(t)

        @pl.when(jnp.logical_not(here))
        def _():
            greet(owner, quad * 2 + t)

        count = count + jnp.where(here, 0, 1)
    for i in range(SLOTS):
        here = (makers[i] == me) & (column == win)

        @pl.when(jnp.logical_not(here))
        def _():
            greet(makers[i], column)

        count = count + jnp.where(here, 0, 1)

    all_blocks = (blocks_0, blocks_1, blocks_2, blocks_3)

    spec_copy.wait()

    def whiten(band, carry):
        cols = pl.ds(pl.multiple_of(band * BAND, BAND), BAND)
        re = spec[0, 0, :, cols]
        im = spec[1, 0, :, cols]
        level = jnp.sum(re * re + im * im, axis=-1, keepdims=True) * (1.0 / BAND)
        scale = lax.rsqrt(level + whiten_eps)
        for part, value in enumerate((re, im)):
            piece = (value * scale).astype(jnp.bfloat16).reshape(BLK, 2, 2, GROUP, BAND)
            for k in range(2):
                for h in range(2):
                    white[k * 2 + h, part * BANDS + band] = piece[:, h, k]
        return carry

    lax.fori_loop(0, BANDS, whiten, 0)

    pl.semaphore_wait(barrier, count)

    def one_copy(part, step):
        to = peer_of(me, step)
        return pltpu.make_async_remote_copy(
            src_ref=white.at[part, to],
            dst_ref=all_blocks[part].at[pl.ds(me * BLK, BLK)],
            send_sem=one_send.at[part, step],
            recv_sem=one_recv.at[part],
            device_id=(to, win),
            device_id_type=MESH,
        )

    def scatter(part):
        def send_one(step, carry):
            one_copy(part, step).start()
            return carry

        lax.fori_loop(1, PAIR, send_one, 0)
        all_blocks[part][pl.ds(me * BLK, BLK)] = white[part, me]

    def scatter_arrived(part):
        most = all_blocks[part].at[pl.ds(0, (PAIR - 1) * BLK)]
        pltpu.make_async_copy(most, most, one_recv.at[part]).wait()

    def pick(n):
        stage, halves = SENDS[n]
        i = stage // 4
        k, role = STAGES[stage % 4]

        def pick_for(step, carry):
            to = z_peer(step)
            for o in range(4):
                for h in halves:
                    outgoing[stage, to, o, h] = all_blocks[k * 2 + h][list_ref[i, role, o * 8 + to]]
            return carry

        lax.fori_loop(1, WIN, pick_for, 0)
        for o in range(4):
            for h in halves:
                plane_in[stage, win, o, h] = all_blocks[k * 2 + h][list_ref[i, role, o * 8 + win]]

    def z_peer(step):
        return lax.rem(win + 4 + step // 2 * (2 * lax.rem(step, 2) - 1), WIN)

    def z_copy(n, step):
        stage, halves = SENDS[n]
        to = z_peer(step)
        whole = len(halves) == 2
        return pltpu.make_async_remote_copy(
            src_ref=outgoing.at[stage, to] if whole else outgoing.at[stage, to, :, halves[0]],
            dst_ref=plane_in.at[stage, win] if whole else plane_in.at[stage, win, :, halves[0]],
            send_sem=z_send.at[n, step],
            recv_sem=z_recv.at[n],
            device_id=(me, to),
            device_id_type=MESH,
        )

    def send_planes(n):
        def send_z(step, carry):
            for before in range(4) if n == 4 else range(n - 1, n) if n > 4 else ():
                z_copy(before, step).wait_send()
            z_copy(n, step).start()
            return carry

        lax.fori_loop(1, WIN, send_z, 0)

    def planes_arrived(stage):
        for n, (of, halves) in enumerate(SENDS):
            if of == stage:
                most = plane_in.at[stage, pl.ds(0, WIN - 1)]
                if len(halves) == 1:
                    most = plane_in.at[stage, pl.ds(0, WIN - 1), :, halves[0]]
                pltpu.make_async_copy(most, most, z_recv.at[n]).wait()

    def spread(stage):
        i = stage // 4
        k, role = STAGES[stage % 4]
        planes_arrived(stage)
        dst = (rcv_in if role else src_in).at[k, me]

        def view(to):
            quad_there = job_of(to, win)[1]
            half = lax.rem(quad_there, 2) if role else quad_there // 2
            return plane_in.at[stage, :, to // 8, half]

        def send_two(step, carry):
            to = peer_of(me, lax.rem(step * 7, PAIR // 2) * 2 + lax.rem(core + i, 2))
            pltpu.make_async_remote_copy(
                src_ref=view(to),
                dst_ref=dst,
                send_sem=two_send.at[stage],
                recv_sem=two_recv.at[stage % 4],
                device_id=(to, win),
                device_id_type=MESH,
            ).start()
            return carry

        @pl.when(core == i)
        def _():
            dst[...] = view(me)[...]

        lax.fori_loop(jnp.where(core == i, 1, 0), PAIR // 2, send_two, 0)

    def arrived(j):
        k, role = STAGES[j]
        most = (rcv_in if role else src_in).at[k, pl.ds(0, PAIR - 1)]
        pltpu.make_async_copy(most, most, two_recv.at[j]).wait()

    def work(unit):
        half, t = unit // 2, unit % 2
        src, rcv = src_in.at[half], rcv_in.at[t]
        here = is_own(t)

        def one_part(e, carry):
            def one_band(band, inner):
                receivers = []
                for w in range(WIN):
                    s_re = src[band, w].astype(jnp.float32)
                    s_im = src[BANDS + band, w].astype(jnp.float32)
                    for n, value in enumerate((s_re, s_im, s_re + s_im)):
                        src_wide[n, w] = value
                    r_re = rcv[band, w].astype(jnp.float32)
                    r_im = rcv[BANDS + band, w].astype(jnp.float32)
                    receivers.append((r_re, r_re + r_im, r_re - r_im))

                for a in range(PART):
                    both = left = right = jnp.zeros((RCV, BAND), jnp.float32)
                    for w in range(WIN):
                        s_re, s_im, s_sum = (
                            jnp.broadcast_to(src_wide[n, w, pl.ds(e * PART + a, 1), :], (RCV, BAND)) for n in range(3)
                        )
                        r_re, r_sum, r_diff = receivers[w]
                        both = both + s_sum * r_re
                        left = left + s_re * r_sum
                        right = right + s_im * r_diff
                    rows = pl.ds(a * RCV, RCV)
                    cols = pl.multiple_of(band * BAND, BAND)
                    cross[rows, pl.ds(cols, BAND)] = (both - right).astype(jnp.bfloat16)
                    cross[rows, pl.ds(NF + cols, BAND)] = (both - left).astype(jnp.bfloat16)
                return inner

            lax.fori_loop(0, BANDS, one_band, 0)
            rows = pl.ds(pl.multiple_of(e * PART * RCV, PART * RCV), PART * RCV)

            def one_tile(tile, inner):
                cols = pl.ds(pl.multiple_of(tile * 512, 512), 512)
                lags = jnp.dot(cross[...], table[:, cols], preferred_element_type=jnp.float32)
                result[unit, rows, cols] = lags.astype(jnp.bfloat16)
                return inner

            lax.fori_loop(0, NLAG // 512, one_tile, 0)

            @pl.when(here)
            def _():
                pltpu.make_async_copy(
                    result.at[unit, rows], out_ref.at[slot, half, rows], back_recv.at[slot, half, e]
                ).start()

            @pl.when(jnp.logical_not(here))
            def _():
                pltpu.make_async_remote_copy(
                    src_ref=result.at[unit, rows],
                    dst_ref=out_ref.at[slot, half, rows],
                    send_sem=back_send.at[unit, e],
                    recv_sem=back_recv.at[slot, half, e],
                    device_id=(owner, quad * 2 + t),
                    device_id_type=MESH,
                ).start()

            return carry

        lax.fori_loop(0, GROUP // PART, one_part, 0)

    def work_after(i, unit, *stages):
        @pl.when(core == i)
        def _():
            for j in stages:
                arrived(j)
            work(unit)

    scatter(0)
    scatter(1)
    scatter_arrived(0)
    pick(0)
    send_planes(0)
    pick(1)
    send_planes(1)
    scatter(2)
    scatter_arrived(1)
    pick(2)
    send_planes(2)
    pick(3)
    send_planes(3)
    scatter(3)
    spread(0)
    scatter_arrived(2)
    scatter_arrived(3)
    pick(4)
    send_planes(4)
    pick(5)
    spread(1)
    send_planes(5)
    pick(6)
    spread(2)
    send_planes(6)
    pick(7)
    spread(3)
    send_planes(7)
    pick(8)
    pick(9)
    table_copy.wait()
    spread(4)
    send_planes(8)
    work_after(0, 0, 0, 1)
    spread(5)
    send_planes(9)
    work_after(0, 1, 2)
    spread(6)
    work_after(0, 2, 3)
    spread(7)
    work_after(0, 3)
    work_after(1, 0, 0, 1)
    work_after(1, 1, 2)
    work_after(1, 2, 3)
    work_after(1, 3)

    def last_sent(step, carry):
        for part in range(4):
            one_copy(part, step).wait_send()
        return carry

    lax.fori_loop(1, PAIR, last_sent, 0)
    for step in range(1, WIN):
        z_copy(9, step).wait_send()
    for stage in range(8):
        for i in range(2):
            @pl.when(lax.rem(core + i, 2) == stage // 4)
            def _():
                sent = src_in.at[0, pl.ds(0, PAIR // 2 - 1 + i)]
                pltpu.make_async_copy(sent, sent, two_send.at[stage]).wait()

    for half in range(2):
        for e in range(GROUP // PART):
            rows = pl.ds(e * PART * RCV, PART * RCV)
            for t in range(2):
                sent = result.at[half * 2 + t, rows]

                @pl.when(jnp.logical_not(is_own(t)))
                def _():
                    pltpu.make_async_copy(sent, sent, back_send.at[half * 2 + t, e]).wait()

            for i in range(SLOTS):
                tile = out_ref.at[i, half, rows]
                pltpu.make_async_copy(tile, tile, back_recv.at[i, half, e]).wait()


def body(spectra, pair_list):
    table = jnp.asarray(lag_table())
    rows = GROUP * RCV
    bf16 = jnp.bfloat16
    dma = pltpu.SemaphoreType.DMA
    out = pl.pallas_call(
        kernel,
        out_shape=jax.ShapeDtypeStruct((SLOTS, 2, rows, NLAG), bf16),
        in_specs=[
            pl.BlockSpec(memory_space=pltpu.SMEM),
            pl.BlockSpec(memory_space=pl.ANY),
            pl.BlockSpec(memory_space=pl.ANY),
        ],
        out_specs=pl.BlockSpec(memory_space=pl.ANY),
        scratch_shapes=[
            pltpu.VMEM((2, 1, BLK * CH, NF), jnp.float32),
            pltpu.VMEM((4, PIECES, BLK, GROUP, BAND), bf16),
            pltpu.VMEM((PAIR * BLK, GROUP, BAND), bf16),
            pltpu.VMEM((PAIR * BLK, GROUP, BAND), bf16),
            pltpu.VMEM((PAIR * BLK, GROUP, BAND), bf16),
            pltpu.VMEM((PAIR * BLK, GROUP, BAND), bf16),
            pltpu.VMEM((8, WIN, 4, 2, GROUP, BAND), bf16),
            pltpu.VMEM((8, WIN, 4, 2, GROUP, BAND), bf16),
            pltpu.VMEM((2, PIECES, WIN, GROUP, BAND), bf16),
            pltpu.VMEM((2, PIECES, WIN, GROUP, BAND), bf16),
            pltpu.VMEM((3, WIN, GROUP, BAND), jnp.float32),
            pltpu.VMEM((PART * RCV, 2 * NF), bf16),
            pltpu.VMEM((2 * NF, NLAG), bf16),
            pltpu.VMEM((4, rows, NLAG), bf16),
            dma, dma,
            dma((4, PAIR)), dma((4,)),
            dma((10, WIN)), dma((10,)),
            dma((8,)), dma((4,)),
            dma((4, GROUP // PART)), dma((SLOTS, 2, GROUP // PART)),
        ],
        compiler_params=pltpu.CompilerParams(
            collective_id=0, has_side_effects=True, vmem_limit_bytes=60 * 1024 * 1024
        ),
    )(pair_list.transpose(1, 2, 0), spectra, table)
    return out.astype(jnp.float32).reshape(SLOTS, 1, SRC, RCV, NLAG)


def solution(mesh):
    in_specs = (P(None, "win", "pair", None), P())
    out_specs = P("pair", "win", None, None, None)
    return jax.shard_map(body, mesh=mesh, in_specs=in_specs, out_specs=out_specs, check_vma=False)
```

```python
import functools

import jax
import jax.numpy as jnp
import ml_dtypes
import numpy as np
from jax import lax
from jax.experimental import pallas as pl
from jax.experimental.pallas import tpu as pltpu
from jax.sharding import PartitionSpec as P

CH = 64
BLK = 3
NF = 2048
BAND = 128
BANDS = NF // BAND
NLAG = 1024
WIN = 8
PAIR = 32
SLOTS = 2
SRC = 32
RCV = 16
PIECES = 2 * BANDS
GROUP = 16
PART = 8
STAGES = [(0, 1), (0, 0), (1, 1), (1, 0)]
SENDS = [(0, (0,)), (1, (0,)), (0, (1,)), (1, (1,))] + [(stage, (0, 1)) for stage in range(2, 8)]
MESH = pl.DeviceIdType.MESH

whiten_eps = 1e-06


def lag_table():
    freqs = np.arange(NF, dtype=np.int64)
    offsets = np.arange(NLAG, dtype=np.int64) - NLAG // 2
    phases = np.mod(freqs[:, None] * np.abs(offsets)[None, :], 2 * NF)
    angles = phases.astype(np.float32) * np.float32(np.pi / NF)
    weights = np.where(freqs == 0, 1.0, 2.0).astype(np.float32) / np.sqrt(np.float32(NF * WIN))
    cos_table = weights[:, None] * np.cos(angles)
    sin_table = -weights[:, None] * (np.sign(offsets).astype(np.float32)[None, :] * np.sin(angles))
    return np.concatenate([cos_table, sin_table], axis=0).astype(ml_dtypes.bfloat16)


def peer_of(me, step):
    y = lax.rem(me // 8 + step // 8, 4)
    x = lax.rem(lax.rem(me // 2, 4) + lax.rem(step // 2, 4), 4)
    core = lax.rem(lax.rem(me, 2) + lax.rem(step, 2), 2)
    return (y * 4 + x) * 2 + core


def job_of(device, win):
    x, core = lax.rem(device // 2, 4), lax.rem(device, 2)
    return core, lax.rem(x + 2 * lax.rem(win + core, 2) + win // 2, 4)


def kernel(
    list_ref, spec_ref, table_ref, out_ref,
    spec, white, blocks_0, blocks_1, blocks_2, blocks_3, outgoing, plane_in, src_in, rcv_in, src_wide, cross, table, result,
    spec_sem, table_sem, one_send, one_recv, z_send, z_recv, two_send, two_recv, back_send, back_recv,
):
    me = lax.axis_index("pair")
    win = lax.axis_index("win")
    row, column = me // 8, lax.rem(me, 8)
    chip, core = me // 2, lax.rem(me, 2)

    spec_copies = []
    for n in range(4):
        lanes = pl.ds(n * NF // 4, NF // 4)
        spec_copies.append(
            pltpu.make_async_copy(spec_ref.at[:, :, :, lanes], spec.at[:, :, :, lanes], spec_sem.at[n])
        )
        spec_copies[n].start()
    table_copy = pltpu.make_async_copy(table_ref, table, table_sem)
    table_copy.start()

    slot, quad = job_of(me, win)
    owner = row * 8 + win

    def is_own(t):
        return (owner == me) & (quad * 2 + t == win)

    shift = win // 2 - column // 2 + 4
    makers = [row * 8 + lax.rem(shift + 2 * lax.rem(column + i, 2), 4) * 2 + i for i in range(SLOTS)]

    barrier = pltpu.get_barrier_semaphore()

    def greet(pair, plane):
        pl.semaphore_signal(barrier, inc=1, device_id=(pair, plane), device_id_type=MESH)

    def greet_pair(step, carry):
        greet(peer_of(me, step), win)
        return carry

    def greet_win(step, carry):
        greet(me, lax.rem(win + step, WIN))
        return carry

    lax.fori_loop(1, PAIR, greet_pair, 0)
    lax.fori_loop(1, WIN, greet_win, 0)
    count = PAIR - 1 + WIN - 1
    for t in range(2):
        here = is_own(t)

        @pl.when(jnp.logical_not(here))
        def _():
            greet(owner, quad * 2 + t)

        count = count + jnp.where(here, 0, 1)
    for i in range(SLOTS):
        here = (makers[i] == me) & (column == win)

        @pl.when(jnp.logical_not(here))
        def _():
            greet(makers[i], column)

        count = count + jnp.where(here, 0, 1)

    all_blocks = (blocks_0, blocks_1, blocks_2, blocks_3)

    def whiten(band, carry):
        cols = pl.ds(pl.multiple_of(band * BAND, BAND), BAND)
        re = spec[0, 0, :, cols]
        im = spec[1, 0, :, cols]
        level = jnp.sum(re * re + im * im, axis=-1, keepdims=True) * (1.0 / BAND)
        scale = lax.rsqrt(level + whiten_eps)
        for part, value in enumerate((re, im)):
            piece = (value * scale).astype(jnp.bfloat16).reshape(BLK, 2, 2, GROUP, BAND)
            for k in range(2):
                for h in range(2):
                    white[k * 2 + h, part * BANDS + band] = piece[:, h, k]
        return carry

    for n in range(4):
        spec_copies[n].wait()
        lax.fori_loop(n * BANDS // 4, (n + 1) * BANDS // 4, whiten, 0)

    pl.semaphore_wait(barrier, count)

    def one_copy(part, step):
        to = peer_of(me, step)
        return pltpu.make_async_remote_copy(
            src_ref=white.at[part, to],
            dst_ref=all_blocks[part].at[pl.ds(me * BLK, BLK)],
            send_sem=one_send.at[part, step],
            recv_sem=one_recv.at[part],
            device_id=(to, win),
            device_id_type=MESH,
        )

    def scatter(part):
        def send_one(step, carry):
            one_copy(part, step).start()
            return carry

        lax.fori_loop(1, PAIR, send_one, 0)
        all_blocks[part][pl.ds(me * BLK, BLK)] = white[part, me]

    def scatter_arrived(part):
        most = all_blocks[part].at[pl.ds(0, (PAIR - 1) * BLK)]
        pltpu.make_async_copy(most, most, one_recv.at[part]).wait()

    def pick(n):
        stage, halves = SENDS[n]
        i = stage // 4
        k, role = STAGES[stage % 4]

        def pick_for(step, carry):
            to = z_peer(step)
            for o in range(4):
                for h in halves:
                    outgoing[stage, to, o, h] = all_blocks[k * 2 + h][list_ref[i, role, o * 8 + to]]
            return carry

        lax.fori_loop(1, WIN, pick_for, 0)
        for o in range(4):
            for h in halves:
                plane_in[stage, win, o, h] = all_blocks[k * 2 + h][list_ref[i, role, o * 8 + win]]

    def z_peer(step):
        return lax.rem(win + 4 + step // 2 * (2 * lax.rem(step, 2) - 1), WIN)

    def z_copy(n, step):
        stage, halves = SENDS[n]
        to = z_peer(step)
        whole = len(halves) == 2
        return pltpu.make_async_remote_copy(
            src_ref=outgoing.at[stage, to] if whole else outgoing.at[stage, to, :, halves[0]],
            dst_ref=plane_in.at[stage, win] if whole else plane_in.at[stage, win, :, halves[0]],
            send_sem=z_send.at[n, step],
            recv_sem=z_recv.at[n],
            device_id=(me, to),
            device_id_type=MESH,
        )

    def send_planes(n):
        def send_z(step, carry):
            for before in range(4) if n == 4 else range(n - 1, n) if n > 4 else ():
                z_copy(before, step).wait_send()
            z_copy(n, step).start()
            return carry

        lax.fori_loop(1, WIN, send_z, 0)

    def planes_arrived(stage):
        for n, (of, halves) in enumerate(SENDS):
            if of == stage:
                most = plane_in.at[stage, pl.ds(0, WIN - 1)]
                if len(halves) == 1:
                    most = plane_in.at[stage, pl.ds(0, WIN - 1), :, halves[0]]
                pltpu.make_async_copy(most, most, z_recv.at[n]).wait()

    def spread(stage):
        i = stage // 4
        k, role = STAGES[stage % 4]
        planes_arrived(stage)
        dst = (rcv_in if role else src_in).at[k, me]

        def view(to):
            quad_there = job_of(to, win)[1]
            half = lax.rem(quad_there, 2) if role else quad_there // 2
            return plane_in.at[stage, :, to // 8, half]

        def send_two(step, carry):
            to = peer_of(me, lax.rem(step * 7, PAIR // 2) * 2 + lax.rem(core + i, 2))
            pltpu.make_async_remote_copy(
                src_ref=view(to),
                dst_ref=dst,
                send_sem=two_send.at[stage],
                recv_sem=two_recv.at[stage % 4],
                device_id=(to, win),
                device_id_type=MESH,
            ).start()
            return carry

        @pl.when(core == i)
        def _():
            dst[...] = view(me)[...]

        lax.fori_loop(jnp.where(core == i, 1, 0), PAIR // 2, send_two, 0)

    def arrived(j):
        k, role = STAGES[j]
        most = (rcv_in if role else src_in).at[k, pl.ds(0, PAIR - 1)]
        pltpu.make_async_copy(most, most, two_recv.at[j]).wait()

    def work(unit):
        half, t = unit // 2, unit % 2
        src, rcv = src_in.at[half], rcv_in.at[t]
        here = is_own(t)

        def one_part(e, carry):
            def one_band(band, inner):
                receivers = []
                for w in range(WIN):
                    s_re = src[band, w].astype(jnp.float32)
                    s_im = src[BANDS + band, w].astype(jnp.float32)
                    for n, value in enumerate((s_re, s_im, s_re + s_im)):
                        src_wide[n, w] = value
                    r_re = rcv[band, w].astype(jnp.float32)
                    r_im = rcv[BANDS + band, w].astype(jnp.float32)
                    receivers.append((r_re, r_re + r_im, r_re - r_im))

                for a in range(PART):
                    both = left = right = jnp.zeros((RCV, BAND), jnp.float32)
                    for w in range(WIN):
                        s_re, s_im, s_sum = (
                            jnp.broadcast_to(src_wide[n, w, pl.ds(e * PART + a, 1), :], (RCV, BAND)) for n in range(3)
                        )
                        r_re, r_sum, r_diff = receivers[w]
                        both = both + s_sum * r_re
                        left = left + s_re * r_sum
                        right = right + s_im * r_diff
                    rows = pl.ds(a * RCV, RCV)
                    cols = pl.multiple_of(band * BAND, BAND)
                    cross[rows, pl.ds(cols, BAND)] = (both - right).astype(jnp.bfloat16)
                    cross[rows, pl.ds(NF + cols, BAND)] = (both - left).astype(jnp.bfloat16)
                return inner

            lax.fori_loop(0, BANDS, one_band, 0)
            rows = pl.ds(pl.multiple_of(e * PART * RCV, PART * RCV), PART * RCV)

            def one_tile(tile, inner):
                cols = pl.ds(pl.multiple_of(tile * 512, 512), 512)
                lags = jnp.dot(cross[...], table[:, cols], preferred_element_type=jnp.float32)
                result[unit, rows, cols] = lags.astype(jnp.bfloat16)
                return inner

            lax.fori_loop(0, NLAG // 512, one_tile, 0)

            @pl.when(here)
            def _():
                pltpu.make_async_copy(
                    result.at[unit, rows], out_ref.at[slot, half, rows], back_recv.at[slot, half, e]
                ).start()

            @pl.when(jnp.logical_not(here))
            def _():
                pltpu.make_async_remote_copy(
                    src_ref=result.at[unit, rows],
                    dst_ref=out_ref.at[slot, half, rows],
                    send_sem=back_send.at[unit, e],
                    recv_sem=back_recv.at[slot, half, e],
                    device_id=(owner, quad * 2 + t),
                    device_id_type=MESH,
                ).start()

            return carry

        lax.fori_loop(0, GROUP // PART, one_part, 0)

    def work_after(i, unit, *stages):
        @pl.when(core == i)
        def _():
            for j in stages:
                arrived(j)
            work(unit)

    scatter(0)
    scatter(1)
    scatter_arrived(0)
    pick(0)
    send_planes(0)
    pick(1)
    send_planes(1)
    scatter(2)
    scatter_arrived(1)
    pick(2)
    send_planes(2)
    pick(3)
    send_planes(3)
    scatter(3)
    spread(0)
    scatter_arrived(2)
    scatter_arrived(3)
    pick(4)
    send_planes(4)
    pick(5)
    spread(1)
    send_planes(5)
    pick(6)
    spread(2)
    send_planes(6)
    pick(7)
    spread(3)
    send_planes(7)
    pick(8)
    pick(9)
    table_copy.wait()
    spread(4)
    send_planes(8)
    work_after(0, 0, 0, 1)
    spread(5)
    send_planes(9)
    work_after(0, 1, 2)
    spread(6)
    work_after(0, 2, 3)
    spread(7)
    work_after(0, 3)
    work_after(1, 0, 0, 1)
    work_after(1, 1, 2)
    work_after(1, 2, 3)
    work_after(1, 3)

    def last_sent(step, carry):
        for part in range(4):
            one_copy(part, step).wait_send()
        return carry

    lax.fori_loop(1, PAIR, last_sent, 0)
    for step in range(1, WIN):
        z_copy(9, step).wait_send()
    for stage in range(8):
        for i in range(2):
            @pl.when(lax.rem(core + i, 2) == stage // 4)
            def _():
                sent = src_in.at[0, pl.ds(0, PAIR // 2 - 1 + i)]
                pltpu.make_async_copy(sent, sent, two_send.at[stage]).wait()

    for half in range(2):
        for e in range(GROUP // PART):
            rows = pl.ds(e * PART * RCV, PART * RCV)
            for t in range(2):
                sent = result.at[half * 2 + t, rows]

                @pl.when(jnp.logical_not(is_own(t)))
                def _():
                    pltpu.make_async_copy(sent, sent, back_send.at[half * 2 + t, e]).wait()

            for i in range(SLOTS):
                tile = out_ref.at[i, half, rows]
                pltpu.make_async_copy(tile, tile, back_recv.at[i, half, e]).wait()


def body(spectra, pair_list):
    table = jnp.asarray(lag_table())
    rows = GROUP * RCV
    bf16 = jnp.bfloat16
    dma = pltpu.SemaphoreType.DMA
    out = pl.pallas_call(
        kernel,
        out_shape=jax.ShapeDtypeStruct((SLOTS, 2, rows, NLAG), bf16),
        in_specs=[
            pl.BlockSpec(memory_space=pltpu.SMEM),
            pl.BlockSpec(memory_space=pl.ANY),
            pl.BlockSpec(memory_space=pl.ANY),
        ],
        out_specs=pl.BlockSpec(memory_space=pl.ANY),
        scratch_shapes=[
            pltpu.VMEM((2, 1, BLK * CH, NF), jnp.float32),
            pltpu.VMEM((4, PIECES, BLK, GROUP, BAND), bf16),
            pltpu.VMEM((PAIR * BLK, GROUP, BAND), bf16),
            pltpu.VMEM((PAIR * BLK, GROUP, BAND), bf16),
            pltpu.VMEM((PAIR * BLK, GROUP, BAND), bf16),
            pltpu.VMEM((PAIR * BLK, GROUP, BAND), bf16),
            pltpu.VMEM((8, WIN, 4, 2, GROUP, BAND), bf16),
            pltpu.VMEM((8, WIN, 4, 2, GROUP, BAND), bf16),
            pltpu.VMEM((2, PIECES, WIN, GROUP, BAND), bf16),
            pltpu.VMEM((2, PIECES, WIN, GROUP, BAND), bf16),
            pltpu.VMEM((3, WIN, GROUP, BAND), jnp.float32),
            pltpu.VMEM((PART * RCV, 2 * NF), bf16),
            pltpu.VMEM((2 * NF, NLAG), bf16),
            pltpu.VMEM((4, rows, NLAG), bf16),
            dma((4,)), dma,
            dma((4, PAIR)), dma((4,)),
            dma((10, WIN)), dma((10,)),
            dma((8,)), dma((4,)),
            dma((4, GROUP // PART)), dma((SLOTS, 2, GROUP // PART)),
        ],
        compiler_params=pltpu.CompilerParams(
            collective_id=0, has_side_effects=True, vmem_limit_bytes=60 * 1024 * 1024
        ),
    )(pair_list.transpose(1, 2, 0), spectra, table)
    return out.astype(jnp.float32).reshape(SLOTS, 1, SRC, RCV, NLAG)


def solution(mesh):
    in_specs = (P(None, "win", "pair", None), P())
    out_specs = P("pair", "win", None, None, None)
    return jax.shard_map(body, mesh=mesh, in_specs=in_specs, out_specs=out_specs, check_vma=False)
```
